512 devices in a mesh: pipe: 16 (over z_hi, x, core), expert: 32 (over y, z_lo).
Axes of the slice: x: 4, y: 8, z: 8 (z_hi: 2, z_lo: 4; z = z_hi * 4 + z_lo), core: 2. Of those that a mesh axis runs over, the one named last changes fastest.
Arguments:
- lead_batch: bfloat16 [16, 2048, 3584], P('pipe', 'expert'), may hold values from -6 to 6
- tail_batch: bfloat16 [16, 2048, 3584], P('pipe', 'expert'), may hold values from -6 to 6
- lead_experts: int32 [16, 2048, 1], P('pipe', 'expert'), may hold values from 0 to 3; in each aligned block of 64 rows (0 to 63, 64 to 127, ..., all dimensions but the last counted through in order) at most 17 rows name the same one
- tail_experts: int32 [16, 2048, 1], P('pipe', 'expert'), may hold values from 0 to 3; in each aligned block of 64 rows (0 to 63, 64 to 127, ..., all dimensions but the last counted through in order) at most 17 rows name the same one
- lead_gates: float32 [16, 2048, 1], P('pipe', 'expert'), may hold values from 0.5 to 1.5
- tail_gates: float32 [16, 2048, 1], P('pipe', 'expert'), may hold values from 0.5 to 1.5
- norm_gain: float32 [16, 3584], P('pipe'), may hold values from 0.1 to 1.9
- gate_proj: bfloat16 [16, 3584, 4096], P('pipe', None, 'expert'), may hold values from -0.09375 to 0.09375
- up_proj: bfloat16 [16, 3584, 4096], P('pipe', None, 'expert'), may hold values from -0.09375 to 0.09375
- down_proj: bfloat16 [16, 4096, 3584], P('pipe', 'expert'), may hold values from -0.1875 to 0.1875
Outputs:
- lead_next: bfloat16 [16, 2048, 3584], P('pipe', 'expert')
- tail_next: bfloat16 [16, 2048, 3584], P('pipe', 'expert')
The draws below stay inside these ranges and needn't reach their ends.
Inputs may be any that keep to these rules, and one draw needn't show every extreme that they name: `lead_experts`: among the 64 tokens of one device in one layer no expert is named more than 17 times, a bound that some block reaches. `tail_experts`: likewise for the tail batch.
All inputs are finite; a program needn't handle non-finite values.
Results may differ from the reference program's by a relative error of at most 0.0095.
Values may be sent and summed in bfloat16 or wider, within the bound.
No kernel may reach another device: no remote copies, remote signals or barrier semaphores. Data moves between devices by JAX's collectives and lax.ppermute only.
A program may use at most 128 MiB of HBM per device.

```python
import math
import jax
import jax.numpy as jnp
import numpy as np
from jax import lax

D = 3584
FF_DEV = 128
EXPERTS = 4
TOP = 1
TOK = 64
CAP = 17
FF = 1024
ROWS = 2048
N_PIPE = 16
N_EXPERT = 32


def block_levels(own_key, shape, cuts, smallest, largest):
    level, own = 1.0, jax.random.fold_in(own_key, 6)
    for axis_at, shards_of in cuts:
        heights = jnp.exp(jax.random.uniform(jax.random.fold_in(own, axis_at), (shards_of,), jnp.float32, smallest / len(cuts), largest / len(cuts)))
        level = level * jnp.repeat(heights, shape[axis_at] // shards_of).reshape([-1 if axis == axis_at else 1 for axis in range(len(shape))])
    return level


def deal_out(stream_key, own, number, rows, number_of, top, bound, slope):
    order = jax.random.permutation(stream_key, number_of)
    heavy_load, usual = portions_of(number_of, rows * top, bound, slope, True), portions_of(number_of, rows * top, bound, slope, False)
    places = jnp.arange(number_of)

    def named(tallies, rotation):
        used = int((tallies > 0).sum())
        fixed = max(1, used // 4)
        shifted = fixed + (places - fixed + rotation * (used - fixed)) % max(1, number_of - fixed)
        return jnp.zeros((number_of,), jnp.int32).at[order[jnp.where(places < fixed, places, shifted)]].set(jnp.asarray(tallies, jnp.int32))

    tallies = jnp.where(number % 4 == 0, named(heavy_load, number // 4), named(usual, number - number // 4 - 1))
    mixed = jax.random.permutation(jax.random.fold_in(own, 3), number_of)
    giver, receiver = mixed[0:number_of // 2 * 2:2], mixed[1:number_of // 2 * 2:2]
    room = jnp.minimum(tallies[giver] - 1, bound - tallies[receiver]) // 2
    room = jnp.where((giver == order[0]) | (receiver == order[0]) | (tallies[receiver] == 0), 0, jnp.maximum(room, 0))
    shifted = jax.random.randint(jax.random.fold_in(own, 4), (number_of // 2,), 0, 1 << 20) % (room + 1)
    tallies = tallies.at[giver].add(-shifted).at[receiver].add(shifted)
    labels = jnp.searchsorted(jnp.cumsum(tallies), jnp.arange(rows * top), side="right").astype(jnp.int32)
    listing = labels.reshape(top, rows).T
    listing = listing[jax.random.permutation(jax.random.fold_in(own, 1), rows)]
    rotation = jax.random.randint(jax.random.fold_in(own, 2), (rows, 1), 0, top)
    return jnp.take_along_axis(listing, (jnp.arange(top)[None, :] + rotation) % top, axis=1)


def portions_of(amount, total, bound, skew, full):
    loads = [(1 << 20) // math.isqrt(grade ** skew) + 1 for grade in range(1, amount + 1)]
    largest = bound if full else min(bound, max(-(-total // amount), total * loads[0] // sum(loads)))
    least = 1 if total - largest >= amount - 1 else 0
    given, surplus = [largest] + [least] * (amount - 1), total - largest - least * (amount - 1)
    while surplus > 0:
        movable = [i for i in range(1, amount) if given[i] < largest] or [i for i in range(1, amount) if given[i] < bound]
        mass, left = sum([loads[i] for i in movable]), surplus
        for i in movable:
            addition = min(bound - given[i], max(1, left * loads[i] // mass), surplus)
            given[i] = given[i] + addition
            surplus = surplus - addition
    return np.array(given)


def gaussian(key, shape, deviation, reach, pieces=(), kind=jnp.bfloat16):
    result = jax.random.normal(key, shape, jnp.float32) * deviation
    if len(pieces) > 0:
        result = block_levels(key, shape, pieces, -0.22, 0.18) * result
    return jnp.clip(result, min=-reach, max=reach).astype(kind)


def setup_inputs(seed: int = 0) -> dict:
    keys = jax.random.split(jax.random.key(seed), 11)
    lead_batch = gaussian(keys[0], (N_PIPE, ROWS, D), 1.0, 6.0, ((0, 16), (1, 32)))
    tail_batch = gaussian(keys[1], (N_PIPE, ROWS, D), 1.0, 6.0, ((0, 16), (1, 32)))
    lead_experts_keys = jax.random.split(jax.random.fold_in(keys[2], 1), N_PIPE * ROWS // TOK)
    lead_experts_turns = jax.random.permutation(jax.random.fold_in(keys[2], 3), N_PIPE * ROWS // TOK)
    lead_experts = jax.vmap(lambda own, number: deal_out(jax.random.fold_in(keys[2], 2), own, number, TOK, EXPERTS, TOP, CAP, 1))(lead_experts_keys, lead_experts_turns).reshape((N_PIPE, ROWS, TOP))
    tail_experts_keys = jax.random.split(jax.random.fold_in(keys[3], 1), N_PIPE * ROWS // TOK)
    tail_experts_turns = jax.random.permutation(jax.random.fold_in(keys[3], 3), N_PIPE * ROWS // TOK)
    tail_experts = jax.vmap(lambda own, number: deal_out(jax.random.fold_in(keys[3], 2), own, number, TOK, EXPERTS, TOP, CAP, 1))(tail_experts_keys, tail_experts_turns).reshape((N_PIPE, ROWS, TOP))
    lead_gates = jnp.clip(0.5 + 1.0 * jax.random.uniform(keys[4], (N_PIPE, ROWS, TOP), jnp.float32) ** block_levels(keys[4], (N_PIPE, ROWS, TOP), ((0, 16), (1, 32)), -0.2, 0.2), 0.5, 1.5)
    tail_gates = jnp.clip(0.5 + 1.0 * jax.random.uniform(keys[5], (N_PIPE, ROWS, TOP), jnp.float32) ** block_levels(keys[5], (N_PIPE, ROWS, TOP), ((0, 16), (1, 32)), -0.2, 0.2), 0.5, 1.5)
    norm_gain = jnp.clip(1.0 + 0.18 * jax.random.normal(keys[6], (N_PIPE, D), jnp.float32), 0.1, 1.9)
    gate_proj = gaussian(keys[7], (N_PIPE, D, EXPERTS * FF), D ** -0.5, 0.09375, ((0, 16), (2, 32)))
    up_proj = gaussian(keys[8], (N_PIPE, D, EXPERTS * FF), D ** -0.5, 0.09375, ((0, 16), (2, 32)))
    down_proj = gaussian(keys[9], (N_PIPE, EXPERTS * FF, D), FF ** -0.5, 0.1875, ((0, 16), (1, 32)))
    return dict(lead_batch=lead_batch, tail_batch=tail_batch, lead_experts=lead_experts, tail_experts=tail_experts, lead_gates=lead_gates, tail_gates=tail_gates, norm_gain=norm_gain, gate_proj=gate_proj, up_proj=up_proj, down_proj=down_proj)


def section_layer(acts, expert_ids, gates, gain, gate_w, up_w, down_w):
    widened = acts.astype(jnp.float32)
    scale = lax.rsqrt(lax.optimization_barrier(jnp.mean(widened * widened, axis=-1, keepdims=True)) + 1e-06)
    normed = (widened * scale * gain.astype(jnp.float32)[None, :]).astype(jnp.bfloat16)
    experts_of = expert_ids[:, 0].astype(jnp.int32)
    route_marks = (experts_of[:, None] == jnp.arange(EXPERTS, dtype=jnp.int32)[None, :]).astype(jnp.int32)
    route_marks = route_marks.reshape(N_EXPERT, TOK, EXPERTS)
    before_count = jnp.cumsum(route_marks, axis=1) - route_marks
    slot_index = lax.optimization_barrier(jnp.sum(before_count * route_marks, axis=-1)).reshape(-1)
    block_index = jnp.arange(N_EXPERT * TOK, dtype=jnp.int32) // TOK
    room = N_EXPERT * CAP
    dest = experts_of * room + block_index * CAP + slot_index
    buffer = jnp.zeros((EXPERTS * room, D), jnp.bfloat16).at[dest].set(normed)
    shards = N_EXPERT // EXPERTS
    results = []
    for expert in range(EXPERTS):
        rows_in = buffer[expert * room:(expert + 1) * room]
        gate_val = jnp.dot(rows_in, gate_w[:, expert * FF:(expert + 1) * FF], preferred_element_type=jnp.float32)
        up_val = jnp.dot(rows_in, up_w[:, expert * FF:(expert + 1) * FF], preferred_element_type=jnp.float32)
        hidden = (jax.nn.silu(gate_val) * up_val).astype(jnp.bfloat16).reshape(room, shards, FF_DEV)
        downs = down_w[expert * FF:(expert + 1) * FF].reshape(shards, FF_DEV, D)
        partial_value = jnp.einsum('nsf,sfd->nsd', hidden.astype(jnp.float32), downs.astype(jnp.float32)).astype(jnp.bfloat16)
        results.append(lax.optimization_barrier(jnp.sum(partial_value.astype(jnp.float32), axis=1)))
    summed = jnp.concatenate(results, axis=0)
    branch = summed[dest]
    return (widened + gates[:, 0:1].astype(jnp.float32) * branch).astype(jnp.bfloat16)

def reference(lead_batch, tail_batch, lead_experts, tail_experts, lead_gates, tail_gates, norm_gain, gate_proj, up_proj, down_proj):

    def run_batch(batch, expert_ids, gates):

        def one_layer(items):
            return section_layer(*items)
        return lax.map(one_layer, (batch, expert_ids, gates, norm_gain, gate_proj, up_proj, down_proj))
    lead_out = run_batch(lead_batch, lead_experts, lead_gates)
    tail_out = run_batch(tail_batch, tail_experts, tail_gates)
    return (jnp.roll(lead_out, 1, axis=0), jnp.roll(tail_out, -1, axis=0))
```

```python
import functools

import jax
import jax.numpy as jnp
from jax import lax
from jax.experimental import pallas as pl
from jax.experimental.pallas import tpu as pltpu
from jax.sharding import PartitionSpec as P

EXPERTS = 4
CAP = 17
MAIN = 16
RUN = 4
D = 3584
TOK = 64
WIDE = 512
GROUPS = D // WIDE
PART = D // RUN
CUT = 128
CUTS = PART // CUT
SENT = MAIN * GROUPS + 8
BACK = MAIN * CUTS + 8
F32 = jnp.float32
BF16 = jnp.bfloat16
PARAMS = pltpu.CompilerParams(vmem_limit_bytes=40 * 1024 * 1024)


def shifted(shard, axis, by):
    size = lax.axis_size(axis)
    return lax.ppermute(shard, axis, [(i, (i + by) % size) for i in range(size)])


def along_run(shard, by):
    size = lax.axis_size("expert")
    return lax.ppermute(
        shard,
        "expert",
        [(i, i // RUN * RUN + (i + by) % RUN) for i in range(size)],
    )


def with_twin(shard):
    size = lax.axis_size("expert")
    return lax.ppermute(shard, "expert", [(i, i ^ RUN) for i in range(size)])


def placing(expert_row):
    kinds = lax.broadcasted_iota(jnp.int32, (8, TOK), 0)
    marks = kinds == expert_row
    earlier = lax.broadcasted_iota(jnp.int32, (TOK, TOK), 0) < lax.broadcasted_iota(
        jnp.int32, (TOK, TOK), 1
    )
    before = jnp.dot(
        marks.astype(F32).astype(BF16),
        earlier.astype(F32).astype(BF16),
        preferred_element_type=F32,
    )
    slot = jnp.sum(jnp.where(marks, before, 0.0), axis=0, keepdims=True).astype(jnp.int32)
    dest = jnp.where(slot < MAIN, expert_row * MAIN + slot, -1)
    main = lax.broadcasted_iota(jnp.int32, (TOK, TOK), 0) == dest
    last = marks & (slot == MAIN)
    return main.astype(F32).astype(BF16), last.astype(F32).astype(BF16)


def spread_kernel(lead_ref, tail_ref, lead_e_ref, tail_e_ref, gain_ref, out_ref, last_ref):
    for j, (x_ref, e_ref) in enumerate(((lead_ref, lead_e_ref), (tail_ref, tail_e_ref))):
        widened = x_ref[...].astype(F32)
        scale = lax.rsqrt(jnp.mean(widened * widened, axis=-1, keepdims=True) + 1e-06)
        normed = (widened * scale * gain_ref[...]).astype(BF16)
        main, last = placing(e_ref[...])
        rows = jnp.dot(main, normed, preferred_element_type=F32).astype(BF16)
        extra = jnp.dot(last, normed, preferred_element_type=F32)
        last_ref[...] = jnp.zeros_like(last_ref)
        for g in range(GROUPS):
            last_ref[:, g, :] = extra[:, g * WIDE : (g + 1) * WIDE]
            for e in range(EXPERTS):
                out_ref[2 * e + j, g * MAIN : (g + 1) * MAIN, :] = rows[
                    e * MAIN : (e + 1) * MAIN, g * WIDE : (g + 1) * WIDE
                ]
        for e in range(EXPERTS):
            out_ref[2 * e + j, GROUPS * MAIN :, :] = last_ref[e].astype(BF16)


def hidden_kernel(x0, x1, x2, x3, ga, gb, ua, ub, out_ref, acc_ref, last_ref):
    parts = (x0, x1, x2, x3)
    senders = x0.shape[0]
    for k, x in enumerate(parts):
        last_ref[k * senders : (k + 1) * senders] = x[:, GROUPS * MAIN :, :].astype(F32)
    for g in range(GROUPS):
        rows = jnp.concatenate(
            [
                x[:, g * MAIN : (g + 1) * MAIN, :].reshape(senders * MAIN, WIDE)
                for x in parts
            ],
            axis=0,
        )
        rows = jnp.concatenate([rows, last_ref[:, g, :].astype(BF16)], axis=0)
        here = pl.ds(g * WIDE, WIDE)
        for n, (g_w, u_w) in enumerate(((ga, ua), (gb, ub))):
            w = jnp.concatenate([g_w[here, :], u_w[here, :]], axis=1)
            got = jnp.dot(rows, w, preferred_element_type=F32)
            cols = slice(n * 256, (n + 1) * 256)
            if g == 0:
                acc_ref[:, cols] = got
            else:
                acc_ref[:, cols] += got
    for n in range(2):
        gate_val = acc_ref[:, n * 256 : n * 256 + 128]
        up_val = acc_ref[:, n * 256 + 128 : n * 256 + 256]
        out_ref[:, n * 128 : (n + 1) * 128] = (jax.nn.silu(gate_val) * up_val).astype(BF16)


def down_kernel(places, h0, h1, h2, h3, a0, a1, a2, a3, b0, b1, b2, b3, out_ref, last_ref):
    senders = 8
    total = None
    full = RUN * senders * MAIN
    for k, (h, a, b) in enumerate(((h0, a0, b0), (h1, a1, b1), (h2, a2, b2), (h3, a3, b3))):
        w = jnp.concatenate([a[...], b[...]], axis=0)
        got = jnp.dot(h[...], w, preferred_element_type=F32)
        at = full - k * senders * MAIN
        end = full + RUN * senders - k * senders
        if k:
            got = jnp.concatenate([got[at:full], got[:at], got[end:], got[full:end]], axis=0)
        total = got if total is None else total + got
    extra = total[full:]
    rows = total[:full].astype(BF16)
    last_ref[...] = jnp.zeros_like(last_ref)
    for c in range(CUTS):
        last_ref[:, c, :] = extra[:, c * CUT : (c + 1) * CUT]
    for k in range(RUN):
        for y in range(senders):
            place = y * RUN + places[k]
            at = k * senders + y
            for c in range(CUTS):
                out_ref[place, c * MAIN : (c + 1) * MAIN, :] = rows[
                    at * MAIN : (at + 1) * MAIN, c * CUT : (c + 1) * CUT
                ]
            out_ref[place, CUTS * MAIN :, :] = last_ref[at].astype(BF16)


def gather_kernel(j, got_ref, x_ref, e_ref, gate_ref, out_ref, rows_ref, last_ref):
    main, last = placing(e_ref[...])
    last_ref[...] = jnp.zeros_like(last_ref)
    for e in range(EXPERTS):
        for r in range(RUN):
            at = (2 * e + j) * RUN + r
            for c in range(CUTS):
                rows_ref[
                    e * MAIN : (e + 1) * MAIN, r * PART + c * CUT : r * PART + (c + 1) * CUT
                ] = got_ref[at, c * MAIN : (c + 1) * MAIN, :]
            last_ref[e, r * 8 : (r + 1) * 8, :] = got_ref[at, CUTS * MAIN :, :].astype(F32)
    extra = jnp.concatenate(
        [last_ref[:, r * 8 + c, :] for r in range(RUN) for c in range(CUTS)], axis=1
    ).astype(BF16)
    over = (((0,), (0,)), ((), ()))
    branch = lax.dot_general(main, rows_ref[...], over, preferred_element_type=F32)
    branch += lax.dot_general(last, extra, over, preferred_element_type=F32)
    out_ref[...] = (x_ref[...].astype(F32) + gate_ref[...] * branch).astype(BF16)


def call(kernel, shape, dtype, scratch, *args, scalars=0):
    specs = [pl.BlockSpec(memory_space=pltpu.SMEM)] * scalars
    specs += [pl.BlockSpec(memory_space=pltpu.VMEM)] * (len(args) - scalars)
    return pl.pallas_call(
        kernel,
        out_shape=jax.ShapeDtypeStruct(shape, dtype),
        in_specs=specs,
        out_specs=pl.BlockSpec(memory_space=pltpu.VMEM),
        scratch_shapes=[pltpu.VMEM(s, t) for s, t in scratch],
        compiler_params=PARAMS,
    )(*args)


def on_device(
    lead_batch,
    tail_batch,
    lead_experts,
    tail_experts,
    lead_gates,
    tail_gates,
    norm_gain,
    gate_proj,
    up_proj,
    down_proj,
):
    size = lax.axis_size("expert")
    senders = size // RUN
    me = lax.axis_index("expert")
    z = me % RUN
    lead_e = lead_experts[0, :, 0][None, :]
    tail_e = tail_experts[0, :, 0][None, :]
    gate_w, up_w, down_w = gate_proj[0], up_proj[0], down_proj[0]

    cut_w = down_w.reshape(down_w.shape[0], RUN, PART)
    mine = [
        lax.dynamic_index_in_dim(cut_w, (z + k) % RUN, axis=1, keepdims=False)
        for k in range(RUN)
    ]
    down_a = [mine[0]] + [along_run(mine[k], k) for k in range(1, RUN)]

    sent = call(
        spread_kernel,
        (2 * EXPERTS, SENT, WIDE),
        BF16,
        [((8, 8, WIDE), F32)],
        lead_batch[0],
        tail_batch[0],
        lead_e,
        tail_e,
        norm_gain,
    )
    columns = [[y * RUN + r for y in range(senders)] for r in range(RUN)]
    own = lax.all_to_all(sent, "expert", 0, 0, axis_index_groups=columns, tiled=True)
    own, gate_w, up_w, down_a = lax.optimization_barrier((own, gate_w, up_w, down_a))
    xs = [own] + [along_run(own, k) for k in range(1, RUN)]
    gate_b, up_b = with_twin(gate_w), with_twin(up_w)
    down_b = [with_twin(w) for w in down_a]
    rows = RUN * senders * CAP
    hidden = call(
        hidden_kernel,
        (rows, 256),
        BF16,
        [
            ((rows, 512), F32),
            ((RUN * senders, 8, WIDE), F32),
        ],
        *xs,
        gate_w,
        gate_b,
        up_w,
        up_b,
    )
    hs = [hidden] + [along_run(hidden, k) for k in range(1, RUN)]
    places = jnp.stack([(z + RUN - k) % RUN for k in range(RUN)]).astype(jnp.int32)
    back = call(
        down_kernel,
        (size, BACK, CUT),
        BF16,
        [((RUN * senders, 8, CUT), F32)],
        places,
        *hs,
        *down_a,
        *down_b,
        scalars=1,
    )
    got = lax.all_to_all(back, "expert", 0, 0, tiled=True)
    outs = []
    for j, (x, e, gates) in enumerate(
        (
            (lead_batch[0], lead_e, lead_gates[0]),
            (tail_batch[0], tail_e, tail_gates[0]),
        )
    ):
        out = call(
            functools.partial(gather_kernel, j),
            (TOK, D),
            BF16,
            [((TOK, D), BF16), ((8, 8 * RUN, CUT), F32)],
            got,
            x,
            e,
            gates,
        )
        outs.append(shifted(out[None], "pipe", 1 if j == 0 else -1))
    return tuple(outs)


def solution(mesh):
    return jax.shard_map(
        on_device,
        mesh=mesh,
        in_specs=(
            P("pipe", "expert", None),
            P("pipe", "expert", None),
            P("pipe", "expert", None),
            P("pipe", "expert", None),
            P("pipe", "expert", None),
            P("pipe", "expert", None),
            P("pipe", None),
            P("pipe", None, "expert"),
            P("pipe", None, "expert"),
            P("pipe", "expert", None),
        ),
        out_specs=(P("pipe", "expert", None), P("pipe", "expert", None)),
        check_vma=False,
    )
```

```python
import functools

import jax
import jax.numpy as jnp
from jax import lax
from jax.experimental import pallas as pl
from jax.experimental.pallas import tpu as pltpu
from jax.sharding import PartitionSpec as P

EXPERTS = 4
CAP = 17
MAIN = 16
RUN = 4
NEAR = 1
TEAM = (0, 4, 2, 6)
D = 3584
TOK = 64
WIDE = 512
GROUPS = D // WIDE
PART = D // RUN
CUT = 128
CUTS = PART // CUT
SENT = MAIN * GROUPS + 8
BACK = MAIN * CUTS + 8
F32 = jnp.float32
BF16 = jnp.bfloat16
PARAMS = pltpu.CompilerParams(vmem_limit_bytes=40 * 1024 * 1024)


def shifted(shard, axis, by):
    size = lax.axis_size(axis)
    return lax.ppermute(shard, axis, [(i, (i + by) % size) for i in range(size)])


def swapped(shard, bits):
    size = lax.axis_size("expert")
    return lax.ppermute(shard, "expert", [(i, i ^ bits) for i in range(size)])


def placing(expert_row):
    kinds = lax.broadcasted_iota(jnp.int32, (8, TOK), 0)
    marks = kinds == expert_row
    earlier = lax.broadcasted_iota(jnp.int32, (TOK, TOK), 0) < lax.broadcasted_iota(
        jnp.int32, (TOK, TOK), 1
    )
    before = jnp.dot(
        marks.astype(F32).astype(BF16),
        earlier.astype(F32).astype(BF16),
        preferred_element_type=F32,
    )
    slot = jnp.sum(jnp.where(marks, before, 0.0), axis=0, keepdims=True).astype(jnp.int32)
    dest = jnp.where(slot < MAIN, expert_row * MAIN + slot, -1)
    main = lax.broadcasted_iota(jnp.int32, (TOK, TOK), 0) == dest
    last = marks & (slot == MAIN)
    return main.astype(F32).astype(BF16), last.astype(F32).astype(BF16)


def spread_kernel(lead_ref, tail_ref, lead_e_ref, tail_e_ref, gain_ref, out_ref, last_ref):
    for j, (x_ref, e_ref) in enumerate(((lead_ref, lead_e_ref), (tail_ref, tail_e_ref))):
        widened = x_ref[...].astype(F32)
        scale = lax.rsqrt(jnp.mean(widened * widened, axis=-1, keepdims=True) + 1e-06)
        normed = (widened * scale * gain_ref[...]).astype(BF16)
        main, last = placing(e_ref[...])
        rows = jnp.dot(main, normed, preferred_element_type=F32).astype(BF16)
        extra = jnp.dot(last, normed, preferred_element_type=F32)
        last_ref[...] = jnp.zeros_like(last_ref)
        for g in range(GROUPS):
            last_ref[:, g, :] = extra[:, g * WIDE : (g + 1) * WIDE]
            for e in range(EXPERTS):
                out_ref[2 * e + j, g * MAIN : (g + 1) * MAIN, :] = rows[
                    e * MAIN : (e + 1) * MAIN, g * WIDE : (g + 1) * WIDE
                ]
        for e in range(EXPERTS):
            out_ref[2 * e + j, GROUPS * MAIN :, :] = last_ref[e].astype(BF16)


def hidden_kernel(*refs):
    *parts, ga, gb, ua, ub, out_ref, acc_ref, last_ref = refs
    at = 0
    for x in parts:
        last_ref[at : at + x.shape[0]] = x[:, GROUPS * MAIN :, :].astype(F32)
        at += x.shape[0]
    for g in range(GROUPS):
        rows = jnp.concatenate(
            [
                x[:, g * MAIN : (g + 1) * MAIN, :].reshape(x.shape[0] * MAIN, WIDE)
                for x in parts
            ],
            axis=0,
        )
        rows = jnp.concatenate([rows, last_ref[:, g, :].astype(BF16)], axis=0)
        here = pl.ds(g * WIDE, WIDE)
        for n, (g_w, u_w) in enumerate(((ga, ua), (gb, ub))):
            w = jnp.concatenate([g_w[here, :], u_w[here, :]], axis=1)
            got = jnp.dot(rows, w, preferred_element_type=F32)
            cols = slice(n * 256, (n + 1) * 256)
            if g == 0:
                acc_ref[:, cols] = got
            else:
                acc_ref[:, cols] += got
    for n in range(2):
        gate_val = acc_ref[:, n * 256 : n * 256 + 128]
        up_val = acc_ref[:, n * 256 + 128 : n * 256 + 256]
        out_ref[:, n * 128 : (n + 1) * 128] = (jax.nn.silu(gate_val) * up_val).astype(BF16)


def down_kernel(places, *refs):
    *hs, wa, wb, out_ref, last_ref = refs
    senders = 8
    total = None
    full = RUN * senders * MAIN
    block = senders * MAIN
    for k in range(RUN):
        w = jnp.concatenate([wa[k], wb[k]], axis=0)
        got = [jnp.dot(h[...], w, preferred_element_type=F32) for h in hs[2 * k : 2 * k + 2]]
        main, last = [], []
        for n in range(RUN):
            m = n ^ k
            at = 2 * block + m % 2 * senders
            main.append(got[m // 2][m % 2 * block : (m % 2 + 1) * block])
            last.append(got[m // 2][at : at + senders])
        got = jnp.concatenate(main + last, axis=0)
        total = got if total is None else total + got
    extra = total[full:]
    rows = total[:full].astype(BF16)
    last_ref[...] = jnp.zeros_like(last_ref)
    for c in range(CUTS):
        last_ref[:, c, :] = extra[:, c * CUT : (c + 1) * CUT]
    for n in range(RUN):
        for y in range(senders):
            place = y * 2 + places[n // 2]
            batch = places[2 + n % 2]
            at = n * senders + y
            for c in range(CUTS):
                out_ref[place, batch, c * MAIN : (c + 1) * MAIN, :] = rows[
                    at * MAIN : (at + 1) * MAIN, c * CUT : (c + 1) * CUT
                ]
            out_ref[place, batch, CUTS * MAIN :, :] = last_ref[at].astype(BF16)


def gather_kernel(j, got_ref, x_ref, e_ref, gate_ref, out_ref, rows_ref, last_ref):
    main, last = placing(e_ref[...])
    last_ref[...] = jnp.zeros_like(last_ref)
    for e in range(EXPERTS):
        for r in range(RUN):
            at = e * RUN + r
            for c in range(CUTS):
                rows_ref[
                    e * MAIN : (e + 1) * MAIN, r * PART + c * CUT : r * PART + (c + 1) * CUT
                ] = got_ref[at, j, c * MAIN : (c + 1) * MAIN, :]
            last_ref[e, r * 8 : (r + 1) * 8, :] = got_ref[at, j, CUTS * MAIN :, :].astype(F32)
    extra = jnp.concatenate(
        [last_ref[:, r * 8 + c, :] for r in range(RUN) for c in range(CUTS)], axis=1
    ).astype(BF16)
    over = (((0,), (0,)), ((), ()))
    branch = lax.dot_general(main, rows_ref[...], over, preferred_element_type=F32)
    branch += lax.dot_general(last, extra, over, preferred_element_type=F32)
    out_ref[...] = (x_ref[...].astype(F32) + gate_ref[...] * branch).astype(BF16)


def call(kernel, shape, dtype, scratch, *args, scalars=0):
    specs = [pl.BlockSpec(memory_space=pltpu.SMEM)] * scalars
    specs += [pl.BlockSpec(memory_space=pltpu.VMEM)] * (len(args) - scalars)
    return pl.pallas_call(
        kernel,
        out_shape=jax.ShapeDtypeStruct(shape, dtype),
        in_specs=specs,
        out_specs=pl.BlockSpec(memory_space=pltpu.VMEM),
        scratch_shapes=[pltpu.VMEM(s, t) for s, t in scratch],
        compiler_params=PARAMS,
    )(*args)


def hidden_of(parts, weights):
    rows = sum(part.shape[0] for part in parts)
    return call(
        hidden_kernel,
        (rows * CAP, 256),
        BF16,
        [((rows * CAP, 512), F32), ((rows, 8, WIDE), F32)],
        *parts,
        *weights,
    )


def on_device(
    lead_batch,
    tail_batch,
    lead_experts,
    tail_experts,
    lead_gates,
    tail_gates,
    norm_gain,
    gate_proj,
    up_proj,
    down_proj,
):
    size = lax.axis_size("expert")
    senders = size // RUN
    me = lax.axis_index("expert")
    twin, far = me // RUN % 2, me % RUN // 2
    lead_e = lead_experts[0, :, 0][None, :]
    tail_e = tail_experts[0, :, 0][None, :]
    gate_w, up_w, down_w = gate_proj[0], up_proj[0], down_proj[0]
    gate_b, up_b = swapped(gate_w, NEAR), swapped(up_w, NEAR)

    cuts = [down_w[:, n * PART : (n + 1) * PART] for n in range(RUN)]
    mine = 2 * twin + far
    parts = []
    for k in range(RUN):
        flip = k % 2 * 2 + k // 2
        parts.append(
            jnp.where(
                mine < 2,
                jnp.where(mine == 0, cuts[flip], cuts[1 ^ flip]),
                jnp.where(mine == 2, cuts[2 ^ flip], cuts[3 ^ flip]),
            )
        )
    from_far = swapped(jnp.stack(parts[2:]), TEAM[2])

    sent = call(
        spread_kernel,
        (2 * EXPERTS, SENT, WIDE),
        BF16,
        [((8, 8, WIDE), F32)],
        lead_batch[0],
        tail_batch[0],
        lead_e,
        tail_e,
        norm_gain,
    )
    columns = [[y * RUN + r for y in range(senders)] for r in range(RUN)]
    own = lax.all_to_all(sent, "expert", 0, 0, axis_index_groups=columns, tiled=True)
    step = lax.optimization_barrier
    own, gate_b, from_far = step((own, gate_b, from_far))
    half = senders // 2
    near_rows, far_rows = swapped(own[:half], TEAM[2]), swapped(own[half:], TEAM[2])
    beside = swapped(own, TEAM[1])
    from_twin = swapped(jnp.stack([parts[1], from_far[1]]), TEAM[1])
    beside, from_twin = step((beside, from_twin))
    weights = (gate_w, gate_b, up_w, up_b)
    early = hidden_of((own, beside), weights)
    down_a = jnp.stack([parts[0], from_twin[0], from_far[0], from_twin[1]])
    early, down_a = step((early, down_a))
    down_b = swapped(down_a, NEAR)
    early_sent = [swapped(early, TEAM[k]) for k in range(1, RUN)]
    near_last, far_last = swapped(near_rows, TEAM[1]), swapped(far_rows, TEAM[1])
    far_last, early_sent = step((far_last, early_sent))
    late = hidden_of((near_rows, far_rows, near_last, far_last), weights)
    hs = [early, late]
    for k in range(1, RUN):
        hs += [early_sent[k - 1], swapped(late, TEAM[k])]
    places = jnp.stack([far, far ^ 1, twin, twin ^ 1]).astype(jnp.int32)
    back = call(
        down_kernel,
        (size // 2, 2, BACK, CUT),
        BF16,
        [((RUN * senders, 8, CUT), F32)],
        places,
        *hs,
        down_a,
        down_b,
        scalars=1,
    )
    halves = [
        [y * RUN + n + 2 * f for y in range(senders) for f in range(2)] for n in range(2)
    ]
    got = lax.all_to_all(back, "expert", 0, 0, axis_index_groups=halves, tiled=True)
    outs = []
    for j, (x, e, gates) in enumerate(
        (
            (lead_batch[0], lead_e, lead_gates[0]),
            (tail_batch[0], tail_e, tail_gates[0]),
        )
    ):
        out = call(
            functools.partial(gather_kernel, j),
            (TOK, D),
            BF16,
            [((TOK, D), BF16), ((8, 8 * RUN, CUT), F32)],
            got,
            x,
            e,
            gates,
        )
        outs.append(shifted(out[None], "pipe", 1 if j == 0 else -1))
    return tuple(outs)


def solution(mesh):
    return jax.shard_map(
        on_device,
        mesh=mesh,
        in_specs=(
            P("pipe", "expert", None),
            P("pipe", "expert", None),
            P("pipe", "expert", None),
            P("pipe", "expert", None),
            P("pipe", "expert", None),
            P("pipe", "expert", None),
            P("pipe", None),
            P("pipe", None, "expert"),
            P("pipe", None, "expert"),
            P("pipe", "expert", None),
        ),
        out_specs=(P("pipe", "expert", None), P("pipe", "expert", None)),
        check_vma=False,
    )
```

```python
import functools

import jax
import jax.numpy as jnp
from jax import lax
from jax.experimental import pallas as pl
from jax.experimental.pallas import tpu as pltpu
from jax.sharding import PartitionSpec as P

EXPERTS = 4
CAP = 17
MAIN = 16
RUN = 4
NEAR = 1
TEAM = (0, 4, 2, 6)
D = 3584
TOK = 64
WIDE = 512
GROUPS = D // WIDE
EARLY = 4 * WIDE
PART = D // RUN
CUT = 128
CUTS = PART // CUT
SENT = MAIN * GROUPS + 8
BACK = MAIN * CUTS + 8
F32 = jnp.float32
BF16 = jnp.bfloat16
PARAMS = pltpu.CompilerParams(vmem_limit_bytes=40 * 1024 * 1024)


def shifted(shard, axis, by):
    size = lax.axis_size(axis)
    return lax.ppermute(shard, axis, [(i, (i + by) % size) for i in range(size)])


def swapped(shard, bits):
    size = lax.axis_size("expert")
    return lax.ppermute(shard, "expert", [(i, i ^ bits) for i in range(size)])


def placing(expert_row):
    kinds = lax.broadcasted_iota(jnp.int32, (8, TOK), 0)
    marks = kinds == expert_row
    earlier = lax.broadcasted_iota(jnp.int32, (TOK, TOK), 0) < lax.broadcasted_iota(
        jnp.int32, (TOK, TOK), 1
    )
    before = jnp.dot(
        marks.astype(F32).astype(BF16),
        earlier.astype(F32).astype(BF16),
        preferred_element_type=F32,
    )
    slot = jnp.sum(jnp.where(marks, before, 0.0), axis=0, keepdims=True).astype(jnp.int32)
    dest = jnp.where(slot < MAIN, expert_row * MAIN + slot, -1)
    main = lax.broadcasted_iota(jnp.int32, (TOK, TOK), 0) == dest
    last = marks & (slot == MAIN)
    return main.astype(F32).astype(BF16), last.astype(F32).astype(BF16)


def spread_kernel(lead_ref, tail_ref, lead_e_ref, tail_e_ref, gain_ref, out_ref, last_ref):
    for j, (x_ref, e_ref) in enumerate(((lead_ref, lead_e_ref), (tail_ref, tail_e_ref))):
        widened = x_ref[...].astype(F32)
        scale = lax.rsqrt(jnp.mean(widened * widened, axis=-1, keepdims=True) + 1e-06)
        normed = (widened * scale * gain_ref[...]).astype(BF16)
        main, last = placing(e_ref[...])
        rows = jnp.dot(main, normed, preferred_element_type=F32).astype(BF16)
        extra = jnp.dot(last, normed, preferred_element_type=F32)
        last_ref[...] = jnp.zeros_like(last_ref)
        for g in range(GROUPS):
            last_ref[:, g, :] = extra[:, g * WIDE : (g + 1) * WIDE]
            for e in range(EXPERTS):
                out_ref[2 * e + j, g * MAIN : (g + 1) * MAIN, :] = rows[
                    e * MAIN : (e + 1) * MAIN, g * WIDE : (g + 1) * WIDE
                ]
        for e in range(EXPERTS):
            out_ref[2 * e + j, GROUPS * MAIN :, :] = last_ref[e].astype(BF16)


def hidden_kernel(*refs):
    *parts, ga, gb_low, gb_high, ua, ub, out_ref, acc_ref, last_ref = refs
    at = 0
    for x in parts:
        last_ref[at : at + x.shape[0]] = x[:, GROUPS * MAIN :, :].astype(F32)
        at += x.shape[0]
    for g in range(GROUPS):
        rows = jnp.concatenate(
            [
                x[:, g * MAIN : (g + 1) * MAIN, :].reshape(x.shape[0] * MAIN, WIDE)
                for x in parts
            ],
            axis=0,
        )
        rows = jnp.concatenate([rows, last_ref[:, g, :].astype(BF16)], axis=0)
        here = pl.ds(g * WIDE, WIDE)
        if g * WIDE < EARLY:
            gb = gb_low[here, :]
        else:
            gb = gb_high[pl.ds(g * WIDE - EARLY, WIDE), :]
        for n, (g_w, u_w) in enumerate(((ga[here, :], ua[here, :]), (gb, ub[here, :]))):
            w = jnp.concatenate([g_w, u_w], axis=1)
            got = jnp.dot(rows, w, preferred_element_type=F32)
            cols = slice(n * 256, (n + 1) * 256)
            if g == 0:
                acc_ref[:, cols] = got
            else:
                acc_ref[:, cols] += got
    for n in range(2):
        gate_val = acc_ref[:, n * 256 : n * 256 + 128]
        up_val = acc_ref[:, n * 256 + 128 : n * 256 + 256]
        out_ref[:, n * 128 : (n + 1) * 128] = (jax.nn.silu(gate_val) * up_val).astype(BF16)


def down_kernel(places, *refs):
    *hs, wa, wb, out_ref, last_ref = refs
    senders = 8
    total = None
    full = RUN * senders * MAIN
    block = senders * MAIN
    for k in range(RUN):
        w = jnp.concatenate([wa[k], wb[k]], axis=0)
        got = [jnp.dot(h[...], w, preferred_element_type=F32) for h in hs[2 * k : 2 * k + 2]]
        main, last = [], []
        for n in range(RUN):
            m = n ^ k
            at = 2 * block + m % 2 * senders
            main.append(got[m // 2][m % 2 * block : (m % 2 + 1) * block])
            last.append(got[m // 2][at : at + senders])
        got = jnp.concatenate(main + last, axis=0)
        total = got if total is None else total + got
    extra = total[full:]
    rows = total[:full].astype(BF16)
    last_ref[...] = jnp.zeros_like(last_ref)
    for c in range(CUTS):
        last_ref[:, c, :] = extra[:, c * CUT : (c + 1) * CUT]
    for n in range(RUN):
        for y in range(senders):
            place = y * 2 + places[n // 2]
            batch = places[2 + n % 2]
            at = n * senders + y
            for c in range(CUTS):
                out_ref[place, batch, c * MAIN : (c + 1) * MAIN, :] = rows[
                    at * MAIN : (at + 1) * MAIN, c * CUT : (c + 1) * CUT
                ]
            out_ref[place, batch, CUTS * MAIN :, :] = last_ref[at].astype(BF16)


def gather_kernel(j, got_ref, x_ref, e_ref, gate_ref, out_ref, rows_ref, last_ref):
    main, last = placing(e_ref[...])
    last_ref[...] = jnp.zeros_like(last_ref)
    for e in range(EXPERTS):
        for r in range(RUN):
            at = e * RUN + r
            for c in range(CUTS):
                rows_ref[
                    e * MAIN : (e + 1) * MAIN, r * PART + c * CUT : r * PART + (c + 1) * CUT
                ] = got_ref[at, j, c * MAIN : (c + 1) * MAIN, :]
            last_ref[e, r * 8 : (r + 1) * 8, :] = got_ref[at, j, CUTS * MAIN :, :].astype(F32)
    extra = jnp.concatenate(
        [last_ref[:, r * 8 + c, :] for r in range(RUN) for c in range(CUTS)], axis=1
    ).astype(BF16)
    over = (((0,), (0,)), ((), ()))
    branch = lax.dot_general(main, rows_ref[...], over, preferred_element_type=F32)
    branch += lax.dot_general(last, extra, over, preferred_element_type=F32)
    out_ref[...] = (x_ref[...].astype(F32) + gate_ref[...] * branch).astype(BF16)


def call(kernel, shape, dtype, scratch, *args, scalars=0):
    specs = [pl.BlockSpec(memory_space=pltpu.SMEM)] * scalars
    specs += [pl.BlockSpec(memory_space=pltpu.VMEM)] * (len(args) - scalars)
    return pl.pallas_call(
        kernel,
        out_shape=jax.ShapeDtypeStruct(shape, dtype),
        in_specs=specs,
        out_specs=pl.BlockSpec(memory_space=pltpu.VMEM),
        scratch_shapes=[pltpu.VMEM(s, t) for s, t in scratch],
        compiler_params=PARAMS,
    )(*args)


def hidden_of(parts, weights):
    rows = sum(part.shape[0] for part in parts)
    return call(
        hidden_kernel,
        (rows * CAP, 256),
        BF16,
        [((rows * CAP, 512), F32), ((rows, 8, WIDE), F32)],
        *parts,
        *weights,
    )


def on_device(
    lead_batch,
    tail_batch,
    lead_experts,
    tail_experts,
    lead_gates,
    tail_gates,
    norm_gain,
    gate_proj,
    up_proj,
    down_proj,
):
    size = lax.axis_size("expert")
    senders = size // RUN
    me = lax.axis_index("expert")
    twin, far = me // RUN % 2, me % RUN // 2
    lead_e = lead_experts[0, :, 0][None, :]
    tail_e = tail_experts[0, :, 0][None, :]
    gate_w, up_w, down_w = gate_proj[0], up_proj[0], down_proj[0]
    gate_low = swapped(gate_w[:EARLY], NEAR)

    cuts = [down_w[:, n * PART : (n + 1) * PART] for n in range(RUN)]
    mine = 2 * twin + far
    parts = []
    for k in range(RUN):
        flip = k % 2 * 2 + k // 2
        parts.append(
            jnp.where(
                mine < 2,
                jnp.where(mine == 0, cuts[flip], cuts[1 ^ flip]),
                jnp.where(mine == 2, cuts[2 ^ flip], cuts[3 ^ flip]),
            )
        )
    from_far = swapped(jnp.stack(parts[2:]), TEAM[2])

    sent = call(
        spread_kernel,
        (2 * EXPERTS, SENT, WIDE),
        BF16,
        [((8, 8, WIDE), F32)],
        lead_batch[0],
        tail_batch[0],
        lead_e,
        tail_e,
        norm_gain,
    )
    columns = [[y * RUN + r for y in range(senders)] for r in range(RUN)]
    own = lax.all_to_all(sent, "expert", 0, 0, axis_index_groups=columns, tiled=True)
    step = lax.optimization_barrier
    own, gate_low, from_far, rest, up_w = step(
        (own, gate_low, from_far, gate_w[EARLY:], up_w)
    )
    gate_high, up_b = swapped(rest, NEAR), swapped(up_w, NEAR)
    far_rows = swapped(own, TEAM[2])
    beside = swapped(own, TEAM[1])
    from_twin = swapped(jnp.stack([parts[1], from_far[1]]), TEAM[1])
    beside, from_twin, up_b, gate_high = step((beside, from_twin, up_b, gate_high))
    weights = (gate_w, gate_low, gate_high, up_w, up_b)
    early = hidden_of((own, beside), weights)
    down_a = jnp.stack([parts[0], from_twin[0], from_far[0], from_twin[1]])
    far_rows, down_a = step((far_rows, down_a))
    down_b = swapped(down_a, NEAR)
    early_sent = [swapped(early, TEAM[k]) for k in range(1, RUN)]
    far_last = swapped(far_rows, TEAM[1])
    far_last, early_sent = step((far_last, early_sent))
    late = hidden_of((far_rows, far_last), weights)
    hs = [early, late]
    for k in range(1, RUN):
        hs += [early_sent[k - 1], swapped(late, TEAM[k])]
    places = jnp.stack([far, far ^ 1, twin, twin ^ 1]).astype(jnp.int32)
    back = call(
        down_kernel,
        (size // 2, 2, BACK, CUT),
        BF16,
        [((RUN * senders, 8, CUT), F32)],
        places,
        *hs,
        down_a,
        down_b,
        scalars=1,
    )
    halves = [
        [y * RUN + n + 2 * f for y in range(senders) for f in range(2)] for n in range(2)
    ]
    got = lax.all_to_all(back, "expert", 0, 0, axis_index_groups=halves, tiled=True)
    outs = []
    for j, (x, e, gates) in enumerate(
        (
            (lead_batch[0], lead_e, lead_gates[0]),
            (tail_batch[0], tail_e, tail_gates[0]),
        )
    ):
        out = call(
            functools.partial(gather_kernel, j),
            (TOK, D),
            BF16,
            [((TOK, D), BF16), ((8, 8 * RUN, CUT), F32)],
            got,
            x,
            e,
            gates,
        )
        outs.append(shifted(out[None], "pipe", 1 if j == 0 else -1))
    return tuple(outs)


def solution(mesh):
    return jax.shard_map(
        on_device,
        mesh=mesh,
        in_specs=(
            P("pipe", "expert", None),
            P("pipe", "expert", None),
            P("pipe", "expert", None),
            P("pipe", "expert", None),
            P("pipe", "expert", None),
            P("pipe", "expert", None),
            P("pipe", None),
            P("pipe", None, "expert"),
            P("pipe", None, "expert"),
            P("pipe", "expert", None),
        ),
        out_specs=(P("pipe", "expert", None), P("pipe", "expert", None)),
        check_vma=False,
    )
```

```python
import functools

import jax
import jax.numpy as jnp
from jax import lax
from jax.experimental import pallas as pl
from jax.experimental.pallas import tpu as pltpu
from jax.sharding import PartitionSpec as P

EXPERTS = 4
CAP = 17
MAIN = 16
RUN = 4
NEAR = 1
TEAM = (0, 4, 2, 6)
D = 3584
TOK = 64
WIDE = 512
GROUPS = D // WIDE
EARLY = 4 * WIDE
PART = D // RUN
CUT = 128
CUTS = PART // CUT
SENT = MAIN * GROUPS + 8
BACK = MAIN * CUTS + 8
F32 = jnp.float32
BF16 = jnp.bfloat16
PARAMS = pltpu.CompilerParams(vmem_limit_bytes=40 * 1024 * 1024)


def shifted(shard, axis, by):
    size = lax.axis_size(axis)
    return lax.ppermute(shard, axis, [(i, (i + by) % size) for i in range(size)])


def swapped(shard, bits):
    size = lax.axis_size("expert")
    return lax.ppermute(shard, "expert", [(i, i ^ bits) for i in range(size)])


def placing(expert_row):
    kinds = lax.broadcasted_iota(jnp.int32, (8, TOK), 0)
    marks = kinds == expert_row
    earlier = lax.broadcasted_iota(jnp.int32, (TOK, TOK), 0) < lax.broadcasted_iota(
        jnp.int32, (TOK, TOK), 1
    )
    before = jnp.dot(
        marks.astype(F32).astype(BF16),
        earlier.astype(F32).astype(BF16),
        preferred_element_type=F32,
    )
    slot = jnp.sum(jnp.where(marks, before, 0.0), axis=0, keepdims=True).astype(jnp.int32)
    dest = jnp.where(slot < MAIN, expert_row * MAIN + slot, -1)
    main = lax.broadcasted_iota(jnp.int32, (TOK, TOK), 0) == dest
    last = marks & (slot == MAIN)
    return main.astype(F32).astype(BF16), last.astype(F32).astype(BF16)


def spread_kernel(lead_ref, tail_ref, lead_e_ref, tail_e_ref, gain_ref, out_ref, last_ref):
    for j, (x_ref, e_ref) in enumerate(((lead_ref, lead_e_ref), (tail_ref, tail_e_ref))):
        widened = x_ref[...].astype(F32)
        scale = lax.rsqrt(jnp.mean(widened * widened, axis=-1, keepdims=True) + 1e-06)
        normed = (widened * scale * gain_ref[...]).astype(BF16)
        main, last = placing(e_ref[...])
        rows = jnp.dot(main, normed, preferred_element_type=F32).astype(BF16)
        extra = jnp.dot(last, normed, preferred_element_type=F32)
        last_ref[...] = jnp.zeros_like(last_ref)
        for g in range(GROUPS):
            last_ref[:, g, :] = extra[:, g * WIDE : (g + 1) * WIDE]
            for e in range(EXPERTS):
                out_ref[2 * e + j, g * MAIN : (g + 1) * MAIN, :] = rows[
                    e * MAIN : (e + 1) * MAIN, g * WIDE : (g + 1) * WIDE
                ]
        for e in range(EXPERTS):
            out_ref[2 * e + j, GROUPS * MAIN :, :] = last_ref[e].astype(BF16)


def hidden_kernel(*refs):
    *parts, ga, gb_low, gb_high, ua, ub, out_ref, acc_ref, last_ref = refs
    at = 0
    for x in parts:
        last_ref[at : at + x.shape[0]] = x[:, GROUPS * MAIN :, :].astype(F32)
        at += x.shape[0]
    for g in range(GROUPS):
        rows = jnp.concatenate(
            [
                x[:, g * MAIN : (g + 1) * MAIN, :].reshape(x.shape[0] * MAIN, WIDE)
                for x in parts
            ],
            axis=0,
        )
        rows = jnp.concatenate([rows, last_ref[:, g, :].astype(BF16)], axis=0)
        here = pl.ds(g * WIDE, WIDE)
        if g * WIDE < EARLY:
            gb = gb_low[here, :]
        else:
            gb = gb_high[pl.ds(g * WIDE - EARLY, WIDE), :]
        for n, (g_w, u_w) in enumerate(((ga[here, :], ua[here, :]), (gb, ub[here, :]))):
            w = jnp.concatenate([g_w, u_w], axis=1)
            got = jnp.dot(rows, w, preferred_element_type=F32)
            cols = slice(n * 256, (n + 1) * 256)
            if g == 0:
                acc_ref[:, cols] = got
            else:
                acc_ref[:, cols] += got
    for n in range(2):
        gate_val = acc_ref[:, n * 256 : n * 256 + 128]
        up_val = acc_ref[:, n * 256 + 128 : n * 256 + 256]
        out_ref[:, n * 128 : (n + 1) * 128] = (jax.nn.silu(gate_val) * up_val).astype(BF16)


def down_kernel(places, *refs):
    *hs, wa, wb, out_ref, last_ref = refs
    senders = 8
    total = None
    full = RUN * senders * MAIN
    block = senders * MAIN
    for k in range(RUN):
        w = jnp.concatenate([wa[k], wb[k]], axis=0)
        got = [jnp.dot(h[...], w, preferred_element_type=F32) for h in hs[2 * k : 2 * k + 2]]
        main, last = [], []
        for n in range(RUN):
            m = n ^ k
            at = 2 * block + m % 2 * senders
            main.append(got[m // 2][m % 2 * block : (m % 2 + 1) * block])
            last.append(got[m // 2][at : at + senders])
        got = jnp.concatenate(main + last, axis=0)
        total = got if total is None else total + got
    extra = total[full:]
    rows = total[:full].astype(BF16)
    last_ref[...] = jnp.zeros_like(last_ref)
    for c in range(CUTS):
        last_ref[:, c, :] = extra[:, c * CUT : (c + 1) * CUT]
    for n in range(RUN):
        for y in range(senders):
            place = y * 2 + places[n // 2]
            batch = places[2 + n % 2]
            at = n * senders + y
            for c in range(CUTS):
                out_ref[place, batch, c * MAIN : (c + 1) * MAIN, :] = rows[
                    at * MAIN : (at + 1) * MAIN, c * CUT : (c + 1) * CUT
                ]
            out_ref[place, batch, CUTS * MAIN :, :] = last_ref[at].astype(BF16)


def gather_kernel(j, got_ref, x_ref, e_ref, gate_ref, out_ref, rows_ref, last_ref):
    main, last = placing(e_ref[...])
    last_ref[...] = jnp.zeros_like(last_ref)
    for e in range(EXPERTS):
        for r in range(RUN):
            at = e * RUN + r
            for c in range(CUTS):
                rows_ref[
                    e * MAIN : (e + 1) * MAIN, r * PART + c * CUT : r * PART + (c + 1) * CUT
                ] = got_ref[at, j, c * MAIN : (c + 1) * MAIN, :]
            last_ref[e, r * 8 : (r + 1) * 8, :] = got_ref[at, j, CUTS * MAIN :, :].astype(F32)
    extra = jnp.concatenate(
        [last_ref[:, r * 8 + c, :] for r in range(RUN) for c in range(CUTS)], axis=1
    ).astype(BF16)
    over = (((0,), (0,)), ((), ()))
    branch = lax.dot_general(main, rows_ref[...], over, preferred_element_type=F32)
    branch += lax.dot_general(last, extra, over, preferred_element_type=F32)
    out_ref[...] = (x_ref[...].astype(F32) + gate_ref[...] * branch).astype(BF16)


def call(kernel, shape, dtype, scratch, *args, scalars=0):
    specs = [pl.BlockSpec(memory_space=pltpu.SMEM)] * scalars
    specs += [pl.BlockSpec(memory_space=pltpu.VMEM)] * (len(args) - scalars)
    return pl.pallas_call(
        kernel,
        out_shape=jax.ShapeDtypeStruct(shape, dtype),
        in_specs=specs,
        out_specs=pl.BlockSpec(memory_space=pltpu.VMEM),
        scratch_shapes=[pltpu.VMEM(s, t) for s, t in scratch],
        compiler_params=PARAMS,
    )(*args)


def hidden_of(parts, weights):
    rows = sum(part.shape[0] for part in parts)
    return call(
        hidden_kernel,
        (rows * CAP, 256),
        BF16,
        [((rows * CAP, 512), F32), ((rows, 8, WIDE), F32)],
        *parts,
        *weights,
    )


def on_device(
    lead_batch,
    tail_batch,
    lead_experts,
    tail_experts,
    lead_gates,
    tail_gates,
    norm_gain,
    gate_proj,
    up_proj,
    down_proj,
):
    size = lax.axis_size("expert")
    senders = size // RUN
    me = lax.axis_index("expert")
    twin, far = me // RUN % 2, me % RUN // 2
    lead_e = lead_experts[0, :, 0][None, :]
    tail_e = tail_experts[0, :, 0][None, :]
    gate_w, up_w, down_w = gate_proj[0], up_proj[0], down_proj[0]
    gate_low = swapped(gate_w[:EARLY], NEAR)

    cuts = [down_w[:, n * PART : (n + 1) * PART] for n in range(RUN)]
    mine = 2 * twin + far
    parts = []
    for k in range(RUN):
        flip = k % 2 * 2 + k // 2
        parts.append(
            jnp.where(
                mine < 2,
                jnp.where(mine == 0, cuts[flip], cuts[1 ^ flip]),
                jnp.where(mine == 2, cuts[2 ^ flip], cuts[3 ^ flip]),
            )
        )
    from_far = swapped(jnp.stack(parts[2:]), TEAM[2])

    sent = call(
        spread_kernel,
        (2 * EXPERTS, SENT, WIDE),
        BF16,
        [((8, 8, WIDE), F32)],
        lead_batch[0],
        tail_batch[0],
        lead_e,
        tail_e,
        norm_gain,
    )
    columns = [[y * RUN + r for y in range(senders)] for r in range(RUN)]
    own = lax.all_to_all(sent, "expert", 0, 0, axis_index_groups=columns, tiled=True)
    step = lax.optimization_barrier
    own, gate_low, from_far, rest, up_w = step(
        (own, gate_low, from_far, gate_w[EARLY:], up_w)
    )
    gate_high, up_b = swapped(rest, NEAR), swapped(up_w, NEAR)
    far_rows = swapped(own, TEAM[2])
    beside = swapped(own, TEAM[1])
    from_twin = swapped(jnp.stack([parts[1], from_far[1]]), TEAM[1])
    beside, from_twin, up_b, gate_high = step((beside, from_twin, up_b, gate_high))
    weights = (gate_w, gate_low, gate_high, up_w, up_b)
    early = hidden_of((own, beside), weights)
    down_a = jnp.stack([parts[0], from_twin[0], from_far[0], from_twin[1]])
    early_sent = [swapped(early, TEAM[k]) for k in range(1, RUN)]
    early_sent[0], down_a = step((early_sent[0], down_a))
    down_b = swapped(down_a, NEAR)
    far_last = swapped(far_rows, TEAM[1])
    far_last, early_sent = step((far_last, early_sent))
    late = hidden_of((far_rows, far_last), weights)
    hs = [early, late]
    for k in range(1, RUN):
        hs += [early_sent[k - 1], swapped(late, TEAM[k])]
    places = jnp.stack([far, far ^ 1, twin, twin ^ 1]).astype(jnp.int32)
    back = call(
        down_kernel,
        (size // 2, 2, BACK, CUT),
        BF16,
        [((RUN * senders, 8, CUT), F32)],
        places,
        *hs,
        down_a,
        down_b,
        scalars=1,
    )
    halves = [
        [y * RUN + n + 2 * f for y in range(senders) for f in range(2)] for n in range(2)
    ]
    got = lax.all_to_all(back, "expert", 0, 0, axis_index_groups=halves, tiled=True)
    outs = []
    for j, (x, e, gates) in enumerate(
        (
            (lead_batch[0], lead_e, lead_gates[0]),
            (tail_batch[0], tail_e, tail_gates[0]),
        )
    ):
        out = call(
            functools.partial(gather_kernel, j),
            (TOK, D),
            BF16,
            [((TOK, D), BF16), ((8, 8 * RUN, CUT), F32)],
            got,
            x,
            e,
            gates,
        )
        outs.append(shifted(out[None], "pipe", 1 if j == 0 else -1))
    return tuple(outs)


def solution(mesh):
    return jax.shard_map(
        on_device,
        mesh=mesh,
        in_specs=(
            P("pipe", "expert", None),
            P("pipe", "expert", None),
            P("pipe", "expert", None),
            P("pipe", "expert", None),
            P("pipe", "expert", None),
            P("pipe", "expert", None),
            P("pipe", None),
            P("pipe", None, "expert"),
            P("pipe", None, "expert"),
            P("pipe", "expert", None),
        ),
        out_specs=(P("pipe", "expert", None), P("pipe", "expert", None)),
        check_vma=False,
    )
```
